32 devices in a mesh: poles: 2 (over y), grid: 16 (over z, x, core).
Axes of the slice: x: 2, y: 2, z: 4, core: 2. Of those that a mesh axis runs over, the one named last changes fastest.
Arguments:
- inverse_block: float32 [2, 2, 1024, 1024], P('poles', None, 'grid'), as said below
- factor_block: float32 [2, 2, 1024, 512], P('poles', None, 'grid'), may hold values from -6 to 6
- diag_inverse: float32 [2, 2, 512, 512], P('poles', None, 'grid'), may hold values from -6 to 6
- residues: float32 [2, 2], P('poles'), may hold values from -4 to 4
- block_owner: int32 [16], replicated, may hold values from 0 to 15, as said below
- row_count: int32 [16], replicated, may hold values from 1 to 64, 768 in all
Outputs:
- density_off: float32 [2, 1024, 512], P(None, 'grid')
- density_diag: float32 [2, 512, 512], P(None, 'grid')
The draws below stay inside these ranges and needn't reach their ends.
Inputs may be any that keep to these rules, and one draw needn't show every extreme that they name: block_owner is a permutation: natural ancestor row block b (natural rows b * 64 to b * 64 + 63) sits at block position block_owner[b] of the arrays split over grid. With its rows put back in natural order, each pole's inverse_block (real part and imaginary part each) is a symmetric matrix.
All inputs are finite; a program needn't handle non-finite values.
Results may differ from the reference program's by a relative error of at most 0.00007.
Values sent between devices are 32-bit elements; how exact they have to be, the bound alone decides.
A program may use at most 128 MiB of HBM per device.

```python
import math
import jax
import jax.numpy as jnp
import numpy as np
from jax import lax

S = 512
RD = 64
NBLK = 16
R = 1024
POLES = 2


def shared_owner(key):
    return jax.random.permutation(jax.random.fold_in(key, 7), NBLK).astype(jnp.int32)


def draw_block_owner(key, part):
    return shared_owner(key)


def draw_inverse_block(key, part):
    owner = shared_owner(key)
    blocks = jnp.arange(NBLK, dtype=jnp.int32)
    inverse_of = jnp.zeros((NBLK,), jnp.int32).at[owner].set(blocks)
    gaussian = jax.random.normal(jax.random.fold_in(key, 11), (POLES, 2, R, R), jnp.float32)
    symmetric = (gaussian + jnp.swapaxes(gaussian, 2, 3)) * (0.5 / R) ** 0.5
    stored = jnp.arange(R, dtype=jnp.int32)
    row_order = inverse_of[stored // RD] * RD + stored % RD
    return symmetric[:, :, row_order, :]


def raised(drawn, stream_key, source, target, parts, factor):
    def block_of(dim):
        return (jnp.arange(drawn.shape[dim]) // (drawn.shape[dim] // parts)).reshape((-1,) + (1,) * (drawn.ndim - 1 - dim))

    first = jax.random.permutation(stream_key, parts)[block_of(target)]
    far = (block_of(target) + parts // 2) % parts
    return jnp.where((block_of(source) == first) | (block_of(source) == far), factor * drawn, drawn)


def levels(stream_key, dims, shards, smallest, high):
    def one(axis_at, shards_of):
        draws = jax.random.uniform(jax.random.fold_in(jax.random.fold_in(stream_key, 6), axis_at), (shards_of,), jnp.float32, smallest / len(shards), high / len(shards))
        return jnp.repeat(jnp.exp(draws), dims[axis_at] // shards_of).reshape((-1,) + (1,) * (len(dims) - axis_at - 1))

    gain = one(*shards[0])
    for cut in shards[1:]:
        gain = gain * one(*cut)
    return gain


def profile(amount, total, limit, slope):
    weights = [(1 << 20) // math.isqrt(rank ** slope) + 1 for rank in range(2, amount + 1)]
    rest, holding = total - limit - (amount - 1), [1] * (amount - 1)
    while rest > 0:
        movable = [i for i in range(amount - 1) if holding[i] < limit]
        pool, remaining = sum([weights[i] for i in movable]), rest
        for i in movable:
            more = min(limit - holding[i], max(1, remaining * weights[i] // pool), rest)
            holding[i] = holding[i] + more
            rest = rest - more
    return np.array([limit] + holding)


def uneven(own_key, amount, total, most, skew):
    if amount == 2:
        one = jax.random.randint(own_key, (), max(1, total - most), min(most, total - 1) + 1)
        return jnp.stack([one, total - one])
    sizes = jnp.asarray(profile(amount, total, most, skew), jnp.int32)
    twos = (amount - 1) // 2
    donor, sink = sizes[1:1 + 2 * twos:2], sizes[2:2 + 2 * twos:2]
    slack = jnp.minimum(donor - 1, most - sink)
    shifted = jax.random.randint(jax.random.fold_in(own_key, 1), (twos,), 0, 1 << 20) % (slack + 1)
    sizes = sizes.at[1:1 + 2 * twos:2].set(donor - shifted).at[2:2 + 2 * twos:2].set(sink + shifted)
    return sizes[jax.random.permutation(jax.random.fold_in(own_key, 2), amount)]


def normal_values(rng, dims, width, reach, shards=(), kind=jnp.bfloat16):
    entries = jax.random.normal(rng, dims, jnp.float32) * width
    if len(shards) > 0:
        entries = levels(rng, dims, shards, -0.22, 0.18) * entries
    return jnp.clip(entries, min=-reach, max=reach).astype(kind)


def heavy_noise(stream_key, extent, deviation, most, cuts, heavy, held_as=jnp.bfloat16):
    entries = deviation * jax.random.normal(stream_key, extent, jnp.float32)
    if cuts:
        entries = entries * levels(stream_key, extent, cuts, -0.22, 0.18)
    return jnp.clip(raised(entries, jax.random.fold_in(stream_key, 3), *heavy), -most, most).astype(held_as)


def setup_inputs(seed: int = 0) -> dict:
    splits = jax.random.split(jax.random.key(seed), 7)
    inverse_block = draw_inverse_block(jax.random.fold_in(splits[6], 71), 0)
    factor_block = heavy_noise(splits[1], (POLES, 2, R, S), 1.0, 6.0, ((0, 2), (2, 16)), (2, 3, 16, 2.0), jnp.float32)
    diag_inverse = normal_values(splits[2], (POLES, 2, S, S), 1.0, 6.0, ((0, 2), (2, 16)), jnp.float32)
    residues = normal_values(splits[3], (POLES, 2), 1.0, 4.0, ((0, 2),), jnp.float32)
    block_owner = draw_block_owner(jax.random.fold_in(splits[6], 71), 0)
    row_count = uneven(splits[5], NBLK, NBLK * RD * 3 // 4, RD, 0).astype(jnp.int32)
    return {"inverse_block": inverse_block, "factor_block": factor_block, "diag_inverse": diag_inverse, "residues": residues, "block_owner": block_owner, "row_count": row_count}


HIGHEST_PRECISION = lax.Precision.HIGHEST


def product(left, right):
    return jnp.dot(left, right, preferred_element_type=jnp.float32, precision=HIGHEST_PRECISION)


def complex_product(left_real, left_imag, right_real, right_imag):
    return (product(left_real, right_real) - product(left_imag, right_imag),
            product(left_real, right_imag) + product(left_imag, right_real))


def weigh(weights, values):
    return jnp.stack([weights[0] * values[0] - weights[1] * values[1],
                      weights[0] * values[1] + weights[1] * values[0]])


def reference(inverse_block, factor_block, diag_inverse, residues, block_owner, row_count):
    blocks = jnp.arange(NBLK, dtype=jnp.int32)
    inverse_of = jnp.zeros((NBLK,), jnp.int32).at[block_owner].set(blocks)
    live_table = (jnp.arange(RD, dtype=jnp.int32)[None, :] < row_count[:, None]).astype(jnp.float32)
    live_rows = live_table[inverse_of].reshape(R)
    masked = factor_block * live_rows[None, None, :, None]
    natural_factor = masked.reshape(POLES, 2, NBLK, RD, S)[:, :, block_owner].reshape(POLES, 2, R, S)

    def one_pole(pole):
        matrix = inverse_block[pole]
        natural_rows = natural_factor[pole]
        masked_rows = masked[pole]
        real_part, imag_part = complex_product(matrix[0], matrix[1], natural_rows[0], natural_rows[1])
        offdiag = -jnp.stack([real_part, imag_part]) * live_rows[None, :, None]
        gram_real, gram_imag = complex_product(masked_rows[0].T, masked_rows[1].T, offdiag[0], offdiag[1])
        diagonal = diag_inverse[pole] - jnp.stack([gram_real, gram_imag])
        return weigh(residues[pole], offdiag), weigh(residues[pole], diagonal)

    offdiags, diagonals = lax.map(one_pole, jnp.arange(POLES, dtype=jnp.int32))
    return jnp.sum(offdiags, axis=0), jnp.sum(diagonals, axis=0)
```

```python
import functools

import jax
import jax.numpy as jnp
from jax import lax
from jax.experimental import pallas as pl
from jax.experimental.pallas import tpu as pltpu
from jax.sharding import PartitionSpec as P

BF16 = jnp.bfloat16
F32 = jnp.float32


def split(values):
    high = values.astype(BF16)
    return high, (values - high.astype(F32)).astype(BF16)


def dot(left, right):
    return jnp.dot(left, right, preferred_element_type=F32)


def pair_product(left4, right_real, right_imag, rows):
    width = right_real.shape[1]
    real_high, real_low = split(right_real)
    imag_high, imag_low = split(right_imag)
    first = dot(left4, jnp.concatenate([real_high, imag_high], axis=1))
    second = dot(left4[: 2 * rows], jnp.concatenate([real_low, imag_low], axis=1))
    by_real = first[: 2 * rows] + first[2 * rows :] + second
    rr, ri = by_real[:rows, :width], by_real[:rows, width:]
    ir, ii = by_real[rows:, :width], by_real[rows:, width:]
    return rr - ii, ri + ir


def nearest(place, step, amount):
    near = jnp.minimum(place, amount - 1 - place)
    half = (step + 1) // 2
    both = jnp.where(step % 2 == 1, place + half, place - half)
    far = jnp.where(place < amount - 1 - place, place + (step - near), place - (step - near))
    return jnp.where(step <= 2 * near, both, far)


def kernel(
    dims, a_ref, f_ref, d_ref, w_ref, owner_ref, count_ref, off_out, diag_out,
    full, a4, off_all, ft, gram, gram_in, pole_off, pole_diag,
    full_send, full_recv, off_send, off_recv, gram_send, gram_recv, po_send, po_recv, pd_send, pd_recv,
):
    poles, outer, inner = dims
    n = outer * inner * 2
    group = inner * 2
    rows, width = f_ref.shape[1], f_ref.shape[2]
    total_rows = a_ref.shape[2]
    share = d_ref.shape[1]
    me = lax.axis_index("grid")
    pole = lax.axis_index("poles")
    z, x, c = me // group, (me // 2) % inner, me % 2

    def index(at_z, at_x, at_c):
        return at_z * group + at_x * 2 + at_c

    barrier = pltpu.get_barrier_semaphore()

    def greet(target):
        pl.semaphore_signal(barrier, inc=1, device_id=target, device_id_type=pl.DeviceIdType.MESH)

    greet((pole, index(z, x, 1 - c)))
    for k in range(1, outer):
        greet((pole, index((z + k) % outer, x, c)))
    for k in range(1, poles):
        greet(((pole + k) % poles, me))
    pl.when(x > 0)(lambda: greet((pole, index(z, x - 1, c))))
    pl.when(x < inner - 1)(lambda: greet((pole, index(z, x + 1, c))))

    live_count = jnp.int32(0)
    for b in range(n):
        live_count = live_count + jnp.where(owner_ref[b] == me, count_ref[b], 0)
    live = (lax.broadcasted_iota(jnp.int32, (rows, width), 0) < live_count).astype(F32)
    full[me, 0] = f_ref[0] * live
    full[me, 1] = f_ref[1] * live

    beside = jnp.where(x > 0, 1, 0) + jnp.where(x < inner - 1, 1, 0)
    pl.semaphore_wait(barrier, outer + poles - 1 + beside)

    def full_copy(slot, way, target):
        return pltpu.make_async_remote_copy(
            src_ref=full.at[slot], dst_ref=full.at[slot],
            send_sem=full_send.at[slot, way], recv_sem=full_recv.at[slot],
            device_id=(pole, target), device_id_type=pl.DeviceIdType.MESH,
        )

    def each_full(from_z, from_x, act):
        slot = index(from_z, from_x, c)
        mine = from_x == x
        pl.when(mine & (z < outer - 1) & (from_z <= z))(lambda: act(full_copy(slot, 0, index(z + 1, x, c))))
        pl.when(mine & (z > 0) & (from_z >= z))(lambda: act(full_copy(slot, 1, index(z - 1, x, c))))
        pl.when((x < inner - 1) & (from_x <= x))(lambda: act(full_copy(slot, 2, index(z, x + 1, c))))
        pl.when((x > 0) & (from_x >= x))(lambda: act(full_copy(slot, 3, index(z, x - 1, c))))
        act(full_copy(slot, 4, index(z, x, 1 - c)))

    each_full(z, x, lambda copy: copy.start())

    real_high, real_low = split(a_ref[0])
    imag_high, imag_low = split(a_ref[1])
    stacked = jnp.concatenate([real_high, imag_high, real_low, imag_low], axis=0)
    chips = outer * inner

    def reorder(chip, carry):
        first, second = jnp.int32(0), jnp.int32(0)
        for b in range(n):
            first = first + jnp.where(owner_ref[b] == 2 * chip, b * rows, 0)
            second = second + jnp.where(owner_ref[b] == 2 * chip + 1, b * rows, 0)
        lane = lax.broadcasted_iota(jnp.int32, (total_rows, 2 * rows), 1)
        wanted = jnp.where(lane < rows, lane + first, lane - rows + second)
        chosen = lax.broadcasted_iota(jnp.int32, (total_rows, 2 * rows), 0) == wanted
        a4[chip] = dot(stacked, chosen.astype(F32).astype(BF16)).astype(BF16)
        return carry

    lax.fori_loop(0, chips, reorder, 0)

    off_all[index(0, x, c)] = jnp.zeros((2, rows, width), F32)

    own = index(0, x, c)

    def diagonal_step(t, carry):
        for i in range(inner):
            j = t - i

            @pl.when((j >= 0) & (j < outer))
            def _():
                from_z = nearest(z, j, outer)
                from_x = nearest(x, jnp.int32(i), inner)

                @pl.when((from_z != z) | (from_x != x))
                def _():
                    full_copy(index(from_z, from_x, c), 4, index(z, x, 1 - c)).wait_recv()
                    each_full(from_z, from_x, lambda copy: copy.start())

        for i in range(inner):
            j = t - 1 - i

            @pl.when((j >= 0) & (j < outer))
            def _():
                from_z = nearest(z, j, outer)
                from_x = nearest(x, jnp.int32(i), inner)
                full_copy(index(from_z, from_x, 1 - c), 4, index(z, x, 1 - c)).wait_recv()
                chip = from_z * inner + from_x
                slot = chip * 2
                right_real = jnp.concatenate([full[slot, 0], full[slot + 1, 0]], axis=0)
                right_imag = jnp.concatenate([full[slot, 1], full[slot + 1, 1]], axis=0)
                real, imag = pair_product(a4[chip], right_real, right_imag, rows)
                off_all[own, 0] = off_all[own, 0] + real
                off_all[own, 1] = off_all[own, 1] + imag

        return carry

    lax.fori_loop(0, outer + inner, diagonal_step, 0)

    off_real = -off_all[own, 0] * live
    off_imag = -off_all[own, 1] * live
    off_all[own, 0] = off_real
    off_all[own, 1] = off_imag

    def off_copy(slot, way, target):
        return pltpu.make_async_remote_copy(
            src_ref=off_all.at[slot], dst_ref=off_all.at[slot],
            send_sem=off_send.at[slot, way], recv_sem=off_recv.at[slot],
            device_id=(pole, target), device_id_type=pl.DeviceIdType.MESH,
        )

    def each_off(from_x, act):
        slot = index(0, from_x, c)
        pl.when((x < inner - 1) & (from_x <= x))(lambda: act(off_copy(slot, 0, index(z, x + 1, c))))
        pl.when((x > 0) & (from_x >= x))(lambda: act(off_copy(slot, 1, index(z, x - 1, c))))
        act(off_copy(slot, 2, index(z, x, 1 - c)))

    each_off(x, lambda copy: copy.start())

    weight_real, weight_imag = w_ref[0], w_ref[1]
    pole_off[pole, 0] = weight_real * off_real - weight_imag * off_imag
    pole_off[pole, 1] = weight_real * off_imag + weight_imag * off_real

    def pole_copy(buffer, send, recv, slot, other, way):
        return pltpu.make_async_remote_copy(
            src_ref=buffer.at[slot], dst_ref=buffer.at[slot],
            send_sem=send.at[way], recv_sem=recv.at[slot],
            device_id=(other, me), device_id_type=pl.DeviceIdType.MESH,
        )

    for k in range(1, poles):
        pole_copy(pole_off, po_send, po_recv, pole, (pole + k) % poles, k).start()

    for chip in range(inner):
        slot = index(z, chip, 0)
        at = slice(chip * 2 * rows, (chip + 1) * 2 * rows)
        for part in range(2):
            ft[part, :, at] = jnp.transpose(jnp.concatenate([full[slot, part], full[slot + 1, part]], axis=0))
    left = []
    for part in range(2):
        left.append(jnp.concatenate(
            [ft[part, pl.ds(pl.multiple_of(index(k, x, c) * share, share), share), :] for k in range(outer)], axis=0))
    left_rh, left_rl = split(left[0])
    left_ih, left_il = split(left[1])
    left4 = jnp.concatenate([left_rh, left_ih, left_rl, left_il], axis=0)

    for i in range(1, inner):
        from_x = nearest(x, jnp.int32(i), inner)
        off_copy(index(0, from_x, c), 2, index(z, x, 1 - c)).wait_recv()
        each_off(from_x, lambda copy: copy.start())
    for i in range(inner):
        off_copy(index(0, i, 1 - c), 2, index(z, x, 1 - c)).wait_recv()

    right_real = jnp.concatenate([off_all[k, 0] for k in range(group)], axis=0)
    right_imag = jnp.concatenate([off_all[k, 1] for k in range(group)], axis=0)
    gram_real, gram_imag = pair_product(left4, right_real, right_imag, outer * share)
    for k in range(outer):
        gram[k, 0] = gram_real[k * share : (k + 1) * share]
        gram[k, 1] = gram_imag[k * share : (k + 1) * share]

    def gram_copy(from_z, to_z, way):
        return pltpu.make_async_remote_copy(
            src_ref=gram.at[to_z], dst_ref=gram_in.at[from_z],
            send_sem=gram_send.at[way], recv_sem=gram_recv.at[from_z],
            device_id=(pole, index(to_z, x, c)), device_id_type=pl.DeviceIdType.MESH,
        )

    for k in range(1, outer):
        gram_copy(z, (z + k) % outer, k).start()
    real, imag = d_ref[0] - gram[z, 0], d_ref[1] - gram[z, 1]
    for k in range(1, outer):
        from_z = (z + k) % outer
        gram_copy(from_z, from_z, k).wait_recv()
        real, imag = real - gram_in[from_z, 0], imag - gram_in[from_z, 1]
    pole_diag[pole, 0] = weight_real * real - weight_imag * imag
    pole_diag[pole, 1] = weight_real * imag + weight_imag * real
    for k in range(1, poles):
        pole_copy(pole_diag, pd_send, pd_recv, pole, (pole + k) % poles, k).start()

    for k in range(1, poles):
        other = (pole + k) % poles
        pole_copy(pole_off, po_send, po_recv, other, other, k).wait_recv()
    total = pole_off[0]
    for k in range(1, poles):
        total = total + pole_off[k]
    off_out[...] = total

    def finish(slot, carry):
        each_full(slot // inner, slot % inner, lambda copy: copy.wait_send())
        return carry

    lax.fori_loop(0, chips, finish, 0)
    for i in range(inner):
        each_off(jnp.int32(i), lambda copy: copy.wait_send())
    for k in range(1, outer):
        gram_copy(z, (z + k) % outer, k).wait_send()
    for k in range(1, poles):
        pole_copy(pole_off, po_send, po_recv, pole, (pole + k) % poles, k).wait_send()
    for k in range(1, poles):
        other = (pole + k) % poles
        pole_copy(pole_diag, pd_send, pd_recv, other, other, k).wait_recv()
    total = pole_diag[0]
    for k in range(1, poles):
        total = total + pole_diag[k]
    diag_out[...] = total
    for k in range(1, poles):
        pole_copy(pole_diag, pd_send, pd_recv, pole, (pole + k) % poles, k).wait_send()


def per_device(dims, inverse_block, factor_block, diag_inverse, residues, block_owner, row_count):
    poles, outer, inner = dims
    _, _, rows, total_rows = inverse_block.shape
    width = factor_block.shape[3]
    share = diag_inverse.shape[2]
    n, group, chips = outer * inner * 2, inner * 2, outer * inner
    dma = pltpu.SemaphoreType.DMA
    vmem, smem = pl.BlockSpec(memory_space=pltpu.VMEM), pl.BlockSpec(memory_space=pltpu.SMEM)
    return pl.pallas_call(
        functools.partial(kernel, dims),
        out_shape=(
            jax.ShapeDtypeStruct((2, rows, width), F32),
            jax.ShapeDtypeStruct((2, share, width), F32),
        ),
        in_specs=[vmem, vmem, vmem, smem, smem, smem],
        out_specs=(vmem, vmem),
        scratch_shapes=[
            pltpu.VMEM((n, 2, rows, width), F32),
            pltpu.VMEM((chips, 4 * rows, 2 * rows), BF16),
            pltpu.VMEM((group, 2, rows, width), F32),
            pltpu.VMEM((2, width, group * rows), F32),
            pltpu.VMEM((outer, 2, share, width), F32),
            pltpu.VMEM((outer, 2, share, width), F32),
            pltpu.VMEM((poles, 2, rows, width), F32),
            pltpu.VMEM((poles, 2, share, width), F32),
            dma((n, 5)), dma((n,)), dma((group, 3)), dma((group,)), dma((outer,)), dma((outer,)),
            dma((poles,)), dma((poles,)), dma((poles,)), dma((poles,)),
        ],
        compiler_params=pltpu.CompilerParams(
            collective_id=0, has_side_effects=True, vmem_limit_bytes=56 * 1024 * 1024
        ),
    )(inverse_block[0], factor_block[0], diag_inverse[0], residues[0], block_owner, row_count)


def grid_lines(mesh):
    chips = mesh.shape["grid"] // 2
    inner = max(k for k in range(1, chips + 1) if chips % k == 0 and k * k <= chips)
    try:
        places = [tuple(device.coords) for device in mesh.devices.reshape(mesh.shape["poles"], -1)[0]][::2]
        moved = next(i for i in range(3) if places[1][i] != places[0][i])
        run = len({place[moved] for place in places})
        inner = run if chips % run == 0 else inner
    except (AttributeError, IndexError, StopIteration):
        pass
    return chips // inner, inner


def solution(mesh):
    placed = (
        P("poles", None, "grid", None),
        P("poles", None, "grid", None),
        P("poles", None, "grid", None),
        P("poles", None),
        P(),
        P(),
    )
    dims = (mesh.shape["poles"],) + grid_lines(mesh)
    return jax.shard_map(
        functools.partial(per_device, dims),
        mesh=mesh,
        in_specs=placed,
        out_specs=(P(None, "grid", None), P(None, "grid", None)),
        check_vma=False,
    )
```

```python
import functools

import jax
import jax.numpy as jnp
from jax import lax
from jax.experimental import pallas as pl
from jax.experimental.pallas import tpu as pltpu
from jax.sharding import PartitionSpec as P

BF16 = jnp.bfloat16
F32 = jnp.float32
SKEW = 2
CHUNKS = 2


def split(values):
    high = values.astype(BF16)
    return high, (values - high.astype(F32)).astype(BF16)


def dot(left, right):
    return jnp.dot(left, right, preferred_element_type=F32)


def pair_product(left4, right_real, right_imag, rows):
    width = right_real.shape[1]
    real_high, real_low = split(right_real)
    imag_high, imag_low = split(right_imag)
    first = dot(left4, jnp.concatenate([real_high, imag_high], axis=1))
    second = dot(left4[: 2 * rows], jnp.concatenate([real_low, imag_low], axis=1))
    by_real = first[: 2 * rows] + first[2 * rows :] + second
    rr, ri = by_real[:rows, :width], by_real[:rows, width:]
    ir, ii = by_real[rows:, :width], by_real[rows:, width:]
    return rr - ii, ri + ir


def nearest(place, step, amount):
    near = jnp.minimum(place, amount - 1 - place)
    half = (step + 1) // 2
    both = jnp.where(step % 2 == 1, place + half, place - half)
    far = jnp.where(place < amount - 1 - place, place + (step - near), place - (step - near))
    return jnp.where(step <= 2 * near, both, far)


def kernel(
    dims, a_ref, f_ref, d_ref, w_ref, owner_ref, count_ref, off_out, diag_out,
    full, a4, off_all, ft, left4, gram, gram_in, pole_off, pole_diag,
    full_send, full_recv, off_send, off_recv, gram_send, gram_recv, po_send, po_recv, pd_send, pd_recv,
):
    poles, outer, inner = dims
    n = outer * inner * 2
    group = inner * 2
    rows, width = f_ref.shape[1], f_ref.shape[2]
    total_rows = a_ref.shape[2]
    share = d_ref.shape[1]
    chunks = full.shape[0]
    wide = width // chunks
    me = lax.axis_index("grid")
    pole = lax.axis_index("poles")
    z, x, c = me // group, (me // 2) % inner, me % 2

    def index(at_z, at_x, at_c):
        return at_z * group + at_x * 2 + at_c

    barrier = pltpu.get_barrier_semaphore()

    def greet(target):
        pl.semaphore_signal(barrier, inc=1, device_id=target, device_id_type=pl.DeviceIdType.MESH)

    greet((pole, index(z, x, 1 - c)))
    for k in range(1, outer):
        greet((pole, index((z + k) % outer, x, c)))
    for k in range(1, poles):
        greet(((pole + k) % poles, me))
    pl.when(x > 0)(lambda: greet((pole, index(z, x - 1, c))))
    pl.when(x < inner - 1)(lambda: greet((pole, index(z, x + 1, c))))

    live_count = jnp.int32(0)
    for b in range(n):
        live_count = live_count + jnp.where(owner_ref[b] == me, count_ref[b], 0)
    live = (lax.broadcasted_iota(jnp.int32, (rows, width), 0) < live_count).astype(F32)
    for h in range(chunks):
        for part in range(2):
            full[h, me, part] = f_ref[part, :, h * wide : (h + 1) * wide] * live[:, :wide]

    beside = jnp.where(x > 0, 1, 0) + jnp.where(x < inner - 1, 1, 0)
    pl.semaphore_wait(barrier, outer + poles - 1 + beside)

    def full_copy(h, slot, way, target):
        return pltpu.make_async_remote_copy(
            src_ref=full.at[h, slot], dst_ref=full.at[h, slot],
            send_sem=full_send.at[h, slot, way], recv_sem=full_recv.at[h, slot],
            device_id=(pole, target), device_id_type=pl.DeviceIdType.MESH,
        )

    def each_full(h, from_z, from_x, act):
        slot = index(from_z, from_x, c)
        mine = from_x == x
        pl.when(mine & (z < outer - 1) & (from_z <= z))(lambda: act(full_copy(h, slot, 0, index(z + 1, x, c))))
        pl.when(mine & (z > 0) & (from_z >= z))(lambda: act(full_copy(h, slot, 1, index(z - 1, x, c))))
        pl.when((x < inner - 1) & (from_x <= x))(lambda: act(full_copy(h, slot, 2, index(z, x + 1, c))))
        pl.when((x > 0) & (from_x >= x))(lambda: act(full_copy(h, slot, 3, index(z, x - 1, c))))
        act(full_copy(h, slot, 4, index(z, x, 1 - c)))

    def start(copy):
        copy.start()

    for h in range(chunks):
        each_full(h, z, x, start)

    real_high, real_low = split(a_ref[0])
    imag_high, imag_low = split(a_ref[1])
    stacked = jnp.concatenate([real_high, imag_high, real_low, imag_low], axis=0)
    chips = outer * inner

    def reorder(chip, carry):
        first, second = jnp.int32(0), jnp.int32(0)
        for b in range(n):
            first = first + jnp.where(owner_ref[b] == 2 * chip, b * rows, 0)
            second = second + jnp.where(owner_ref[b] == 2 * chip + 1, b * rows, 0)
        lane = lax.broadcasted_iota(jnp.int32, (total_rows, 2 * rows), 1)
        wanted = jnp.where(lane < rows, lane + first, lane - rows + second)
        chosen = lax.broadcasted_iota(jnp.int32, (total_rows, 2 * rows), 0) == wanted
        a4[chip] = dot(stacked, chosen.astype(F32).astype(BF16)).astype(BF16)
        return carry

    lax.fori_loop(0, chips, reorder, 0)

    own = index(0, x, c)

    def make_rows():
        for h in range(chunks):
            for chip in range(inner):
                slot = index(z, chip, 0)
                at = slice(chip * 2 * rows, (chip + 1) * 2 * rows)
                for part in range(2):
                    ft[part, h * wide : (h + 1) * wide, at] = jnp.transpose(
                        jnp.concatenate([full[h, slot, part], full[h, slot + 1, part]], axis=0))
        left = []
        for part in range(2):
            left.append(jnp.concatenate(
                [ft[part, pl.ds(pl.multiple_of(index(k, x, c) * share, share), share), :] for k in range(outer)],
                axis=0))
        left_rh, left_rl = split(left[0])
        left_ih, left_il = split(left[1])
        left4[...] = jnp.concatenate([left_rh, left_ih, left_rl, left_il], axis=0)

    weight_real, weight_imag = w_ref[0], w_ref[1]

    def off_copy(h, slot, way, target):
        return pltpu.make_async_remote_copy(
            src_ref=off_all.at[h, slot], dst_ref=off_all.at[h, slot],
            send_sem=off_send.at[h, slot, way], recv_sem=off_recv.at[h, slot],
            device_id=(pole, target), device_id_type=pl.DeviceIdType.MESH,
        )

    def each_off(h, from_x, act):
        slot = index(0, from_x, c)
        pl.when((x < inner - 1) & (from_x <= x))(lambda: act(off_copy(h, slot, 0, index(z, x + 1, c))))
        pl.when((x > 0) & (from_x >= x))(lambda: act(off_copy(h, slot, 1, index(z, x - 1, c))))
        act(off_copy(h, slot, 2, index(z, x, 1 - c)))

    def pole_copy(h, buffer, send, recv, slot, other, way):
        return pltpu.make_async_remote_copy(
            src_ref=buffer.at[h, slot], dst_ref=buffer.at[h, slot],
            send_sem=send.at[h, way], recv_sem=recv.at[h, slot],
            device_id=(other, me), device_id_type=pl.DeviceIdType.MESH,
        )

    def gram_copy(h, from_z, to_z, way):
        return pltpu.make_async_remote_copy(
            src_ref=gram.at[h, to_z], dst_ref=gram_in.at[h, from_z],
            send_sem=gram_send.at[h, way], recv_sem=gram_recv.at[h, from_z],
            device_id=(pole, index(to_z, x, c)), device_id_type=pl.DeviceIdType.MESH,
        )

    last = outer + inner - 1
    for h in range(chunks):
        off_all[h, own] = jnp.zeros((2, rows, wide), F32)

    def relay(h, t):
        for i in range(inner):
            j = t - i

            @pl.when((j >= 0) & (j < outer) & (t > 0))
            def _():
                from_z = nearest(z, j, outer)
                from_x = nearest(x, jnp.int32(i), inner)
                full_copy(h, index(from_z, from_x, c), 4, index(z, x, 1 - c)).wait_recv()
                each_full(h, from_z, from_x, start)

    def multiply(h, t):
        for i in range(inner):
            j = t - 1 - i

            @pl.when((j >= 0) & (j < outer))
            def _():
                from_z = nearest(z, j, outer)
                from_x = nearest(x, jnp.int32(i), inner)
                full_copy(h, index(from_z, from_x, 1 - c), 4, index(z, x, 1 - c)).wait_recv()
                chip = from_z * inner + from_x
                slot = chip * 2
                right_real = jnp.concatenate([full[h, slot, 0], full[h, slot + 1, 0]], axis=0)
                right_imag = jnp.concatenate([full[h, slot, 1], full[h, slot + 1, 1]], axis=0)
                real, imag = pair_product(a4[chip], right_real, right_imag, rows)
                off_all[h, own, 0] = off_all[h, own, 0] + real
                off_all[h, own, 1] = off_all[h, own, 1] + imag

    def gather(first):
        def step(t, carry):
            for h in range(first, chunks):
                relay(h, t - SKEW * h)
            for h in range(first, chunks):
                multiply(h, t - SKEW * h)
            return carry

        begin = 1 if first == 0 else last + 1 + SKEW * (first - 1)
        lax.fori_loop(begin, last + 1 + SKEW * first, step, 0)

    def finish_rows(h):
        off_real = -off_all[h, own, 0] * live[:, :wide]
        off_imag = -off_all[h, own, 1] * live[:, :wide]
        off_all[h, own, 0] = off_real
        off_all[h, own, 1] = off_imag
        each_off(h, x, start)
        pole_off[h, pole, 0] = weight_real * off_real - weight_imag * off_imag
        pole_off[h, pole, 1] = weight_real * off_imag + weight_imag * off_real
        for k in range(1, poles):
            pole_copy(h, pole_off, po_send, po_recv, pole, (pole + k) % poles, k).start()

    def make_gram(h):
        for i in range(1, inner):
            from_x = nearest(x, jnp.int32(i), inner)
            off_copy(h, index(0, from_x, c), 2, index(z, x, 1 - c)).wait_recv()
            each_off(h, from_x, start)
        for i in range(inner):
            off_copy(h, index(0, i, 1 - c), 2, index(z, x, 1 - c)).wait_recv()
        right_real = jnp.concatenate([off_all[h, k, 0] for k in range(group)], axis=0)
        right_imag = jnp.concatenate([off_all[h, k, 1] for k in range(group)], axis=0)
        gram_real, gram_imag = pair_product(left4[...], right_real, right_imag, outer * share)
        for k in range(outer):
            gram[h, k, 0] = gram_real[k * share : (k + 1) * share]
            gram[h, k, 1] = gram_imag[k * share : (k + 1) * share]
        for k in range(1, outer):
            gram_copy(h, z, (z + k) % outer, k).start()

    def sum_gram(h):
        at = slice(h * wide, (h + 1) * wide)
        real, imag = d_ref[0, :, at] - gram[h, z, 0], d_ref[1, :, at] - gram[h, z, 1]
        for k in range(1, outer):
            from_z = (z + k) % outer
            gram_copy(h, from_z, from_z, k).wait_recv()
            real, imag = real - gram_in[h, from_z, 0], imag - gram_in[h, from_z, 1]
        pole_diag[h, pole, 0] = weight_real * real - weight_imag * imag
        pole_diag[h, pole, 1] = weight_real * imag + weight_imag * real
        for k in range(1, poles):
            pole_copy(h, pole_diag, pd_send, pd_recv, pole, (pole + k) % poles, k).start()

    for h in range(chunks + 2):
        if h < chunks:
            gather(h)
            finish_rows(h)
        if h == 1:
            make_rows()
        if 1 <= h <= chunks:
            make_gram(h - 1)
        if h >= 2:
            sum_gram(h - 2)

    def add_poles(h, buffer, send, recv, out):
        for k in range(1, poles):
            other = (pole + k) % poles
            pole_copy(h, buffer, send, recv, other, other, k).wait_recv()
        total = buffer[h, 0]
        for k in range(1, poles):
            total = total + buffer[h, k]
        out[:, :, h * wide : (h + 1) * wide] = total

    for h in range(chunks):
        add_poles(h, pole_off, po_send, po_recv, off_out)

    def finish(slot, carry):
        for h in range(chunks):
            each_full(h, slot // inner, slot % inner, lambda copy: copy.wait_send())
        return carry

    lax.fori_loop(0, chips, finish, 0)
    for h in range(chunks):
        for i in range(inner):
            each_off(h, jnp.int32(i), lambda copy: copy.wait_send())
        for k in range(1, outer):
            gram_copy(h, z, (z + k) % outer, k).wait_send()
        for k in range(1, poles):
            pole_copy(h, pole_off, po_send, po_recv, pole, (pole + k) % poles, k).wait_send()
    for h in range(chunks):
        add_poles(h, pole_diag, pd_send, pd_recv, diag_out)
        for k in range(1, poles):
            pole_copy(h, pole_diag, pd_send, pd_recv, pole, (pole + k) % poles, k).wait_send()


def per_device(dims, inverse_block, factor_block, diag_inverse, residues, block_owner, row_count):
    poles, outer, inner = dims
    _, _, rows, total_rows = inverse_block.shape
    width = factor_block.shape[3]
    share = diag_inverse.shape[2]
    n, group, chips = outer * inner * 2, inner * 2, outer * inner
    dma = pltpu.SemaphoreType.DMA
    chunks = CHUNKS if width % (128 * CHUNKS) == 0 else 1
    wide = width // chunks
    vmem, smem = pl.BlockSpec(memory_space=pltpu.VMEM), pl.BlockSpec(memory_space=pltpu.SMEM)
    return pl.pallas_call(
        functools.partial(kernel, dims),
        out_shape=(
            jax.ShapeDtypeStruct((2, rows, width), F32),
            jax.ShapeDtypeStruct((2, share, width), F32),
        ),
        in_specs=[vmem, vmem, vmem, smem, smem, smem],
        out_specs=(vmem, vmem),
        scratch_shapes=[
            pltpu.VMEM((chunks, n, 2, rows, wide), F32),
            pltpu.VMEM((chips, 4 * rows, 2 * rows), BF16),
            pltpu.VMEM((chunks, group, 2, rows, wide), F32),
            pltpu.VMEM((2, width, group * rows), F32),
            pltpu.VMEM((4 * outer * share, group * rows), BF16),
            pltpu.VMEM((chunks, outer, 2, share, wide), F32),
            pltpu.VMEM((chunks, outer, 2, share, wide), F32),
            pltpu.VMEM((chunks, poles, 2, rows, wide), F32),
            pltpu.VMEM((chunks, poles, 2, share, wide), F32),
            dma((chunks, n, 5)), dma((chunks, n)), dma((chunks, group, 3)), dma((chunks, group)),
            dma((chunks, outer)), dma((chunks, outer)),
            dma((chunks, poles)), dma((chunks, poles)), dma((chunks, poles)), dma((chunks, poles)),
        ],
        compiler_params=pltpu.CompilerParams(
            collective_id=0, has_side_effects=True, vmem_limit_bytes=56 * 1024 * 1024
        ),
    )(inverse_block[0], factor_block[0], diag_inverse[0], residues[0], block_owner, row_count)


def grid_lines(mesh):
    chips = mesh.shape["grid"] // 2
    inner = max(k for k in range(1, chips + 1) if chips % k == 0 and k * k <= chips)
    try:
        places = [tuple(device.coords) for device in mesh.devices.reshape(mesh.shape["poles"], -1)[0]][::2]
        moved = next(i for i in range(3) if places[1][i] != places[0][i])
        run = len({place[moved] for place in places})
        inner = run if chips % run == 0 else inner
    except (AttributeError, IndexError, StopIteration):
        pass
    return chips // inner, inner


def solution(mesh):
    placed = (
        P("poles", None, "grid", None),
        P("poles", None, "grid", None),
        P("poles", None, "grid", None),
        P("poles", None),
        P(),
        P(),
    )
    dims = (mesh.shape["poles"],) + grid_lines(mesh)
    return jax.shard_map(
        functools.partial(per_device, dims),
        mesh=mesh,
        in_specs=placed,
        out_specs=(P(None, "grid", None), P(None, "grid", None)),
        check_vma=False,
    )
```

```python
import functools

import jax
import jax.numpy as jnp
from jax import lax
from jax.experimental import pallas as pl
from jax.experimental.pallas import tpu as pltpu
from jax.sharding import PartitionSpec as P

BF16 = jnp.bfloat16
F32 = jnp.float32
SKEW = 2
LAG = 2
CHUNKS = 2


def split(values):
    high = values.astype(BF16)
    return high, (values - high.astype(F32)).astype(BF16)


def dot(left, right):
    return jnp.dot(left, right, preferred_element_type=F32)


def pair_product(left4, right_real, right_imag, rows):
    width = right_real.shape[1]
    real_high, real_low = split(right_real)
    imag_high, imag_low = split(right_imag)
    first = dot(left4, jnp.concatenate([real_high, imag_high], axis=1))
    second = dot(left4[: 2 * rows], jnp.concatenate([real_low, imag_low], axis=1))
    by_real = first[: 2 * rows] + first[2 * rows :] + second
    rr, ri = by_real[:rows, :width], by_real[:rows, width:]
    ir, ii = by_real[rows:, :width], by_real[rows:, width:]
    return rr - ii, ri + ir


def nearest(place, step, amount):
    near = jnp.minimum(place, amount - 1 - place)
    half = (step + 1) // 2
    both = jnp.where(step % 2 == 1, place + half, place - half)
    far = jnp.where(place < amount - 1 - place, place + (step - near), place - (step - near))
    return jnp.where(step <= 2 * near, both, far)


def kernel(
    dims, a_ref, f_ref, d_ref, w_ref, owner_ref, count_ref, off_out, diag_out,
    full, a4, off_all, ft, left4, gram, gram_in, pole_off, pole_diag,
    full_send, full_recv, off_send, off_recv, gram_send, gram_recv, po_send, po_recv, pd_send, pd_recv,
):
    poles, outer, inner = dims
    n = outer * inner * 2
    group = inner * 2
    rows, width = f_ref.shape[1], f_ref.shape[2]
    total_rows = a_ref.shape[2]
    share = d_ref.shape[1]
    chunks = full.shape[0]
    wide = width // chunks
    me = lax.axis_index("grid")
    pole = lax.axis_index("poles")
    z, x, c = me // group, (me // 2) % inner, me % 2

    def index(at_z, at_x, at_c):
        return at_z * group + at_x * 2 + at_c

    barrier = pltpu.get_barrier_semaphore()

    def greet(target):
        pl.semaphore_signal(barrier, inc=1, device_id=target, device_id_type=pl.DeviceIdType.MESH)

    greet((pole, index(z, x, 1 - c)))
    for k in range(1, outer):
        greet((pole, index((z + k) % outer, x, c)))
    for k in range(1, poles):
        greet(((pole + k) % poles, me))
    pl.when(x > 0)(lambda: greet((pole, index(z, x - 1, c))))
    pl.when(x < inner - 1)(lambda: greet((pole, index(z, x + 1, c))))

    live_count = jnp.int32(0)
    for b in range(n):
        live_count = live_count + jnp.where(owner_ref[b] == me, count_ref[b], 0)
    live = (lax.broadcasted_iota(jnp.int32, (rows, width), 0) < live_count).astype(F32)
    for h in range(chunks):
        for part in range(2):
            full[h, me, part] = f_ref[part, :, h * wide : (h + 1) * wide] * live[:, :wide]

    beside = jnp.where(x > 0, 1, 0) + jnp.where(x < inner - 1, 1, 0)
    pl.semaphore_wait(barrier, outer + poles - 1 + beside)

    def full_copy(h, slot, way, target):
        return pltpu.make_async_remote_copy(
            src_ref=full.at[h, slot], dst_ref=full.at[h, slot],
            send_sem=full_send.at[h, slot, way], recv_sem=full_recv.at[h, slot],
            device_id=(pole, target), device_id_type=pl.DeviceIdType.MESH,
        )

    def each_full(h, from_z, from_x, act):
        slot = index(from_z, from_x, c)
        mine = from_x == x
        pl.when(mine & (z < outer - 1) & (from_z <= z))(lambda: act(full_copy(h, slot, 0, index(z + 1, x, c))))
        pl.when(mine & (z > 0) & (from_z >= z))(lambda: act(full_copy(h, slot, 1, index(z - 1, x, c))))
        pl.when((x < inner - 1) & (from_x <= x))(lambda: act(full_copy(h, slot, 2, index(z, x + 1, c))))
        pl.when((x > 0) & (from_x >= x))(lambda: act(full_copy(h, slot, 3, index(z, x - 1, c))))
        act(full_copy(h, slot, 4, index(z, x, 1 - c)))

    def start(copy):
        copy.start()

    for h in range(chunks):
        each_full(h, z, x, start)

    real_high, real_low = split(a_ref[0])
    imag_high, imag_low = split(a_ref[1])
    stacked = jnp.concatenate([real_high, imag_high, real_low, imag_low], axis=0)
    chips = outer * inner

    def reorder(chip, carry):
        first, second = jnp.int32(0), jnp.int32(0)
        for b in range(n):
            first = first + jnp.where(owner_ref[b] == 2 * chip, b * rows, 0)
            second = second + jnp.where(owner_ref[b] == 2 * chip + 1, b * rows, 0)
        lane = lax.broadcasted_iota(jnp.int32, (total_rows, 2 * rows), 1)
        wanted = jnp.where(lane < rows, lane + first, lane - rows + second)
        chosen = lax.broadcasted_iota(jnp.int32, (total_rows, 2 * rows), 0) == wanted
        a4[chip] = dot(stacked, chosen.astype(F32).astype(BF16)).astype(BF16)
        return carry

    lax.fori_loop(0, chips, reorder, 0)

    own = index(0, x, c)

    def make_rows():
        for h in range(chunks):
            for chip in range(inner):
                slot = index(z, chip, 0)
                at = slice(chip * 2 * rows, (chip + 1) * 2 * rows)
                for part in range(2):
                    ft[part, h * wide : (h + 1) * wide, at] = jnp.transpose(
                        jnp.concatenate([full[h, slot, part], full[h, slot + 1, part]], axis=0))
        left = []
        for part in range(2):
            left.append(jnp.concatenate(
                [ft[part, pl.ds(pl.multiple_of(index(k, x, c) * share, share), share), :] for k in range(outer)],
                axis=0))
        left_rh, left_rl = split(left[0])
        left_ih, left_il = split(left[1])
        left4[...] = jnp.concatenate([left_rh, left_ih, left_rl, left_il], axis=0)

    weight_real, weight_imag = w_ref[0], w_ref[1]

    def off_copy(h, slot, way, target):
        return pltpu.make_async_remote_copy(
            src_ref=off_all.at[h, slot], dst_ref=off_all.at[h, slot],
            send_sem=off_send.at[h, slot, way], recv_sem=off_recv.at[h, slot],
            device_id=(pole, target), device_id_type=pl.DeviceIdType.MESH,
        )

    def each_off(h, from_x, act):
        slot = index(0, from_x, c)
        pl.when((x < inner - 1) & (from_x <= x))(lambda: act(off_copy(h, slot, 0, index(z, x + 1, c))))
        pl.when((x > 0) & (from_x >= x))(lambda: act(off_copy(h, slot, 1, index(z, x - 1, c))))
        act(off_copy(h, slot, 2, index(z, x, 1 - c)))

    def pole_copy(h, buffer, send, recv, slot, other, way):
        return pltpu.make_async_remote_copy(
            src_ref=buffer.at[h, slot], dst_ref=buffer.at[h, slot],
            send_sem=send.at[h, way], recv_sem=recv.at[h, slot],
            device_id=(other, me), device_id_type=pl.DeviceIdType.MESH,
        )

    def gram_copy(h, from_z, to_z, way):
        return pltpu.make_async_remote_copy(
            src_ref=gram.at[h, to_z], dst_ref=gram_in.at[h, from_z],
            send_sem=gram_send.at[h, way], recv_sem=gram_recv.at[h, from_z],
            device_id=(pole, index(to_z, x, c)), device_id_type=pl.DeviceIdType.MESH,
        )

    last = outer + LAG * (inner - 1)
    for h in range(chunks):
        off_all[h, own] = jnp.zeros((2, rows, wide), F32)

    def relay(h, t):
        for i in range(inner):
            j = t - LAG * i

            @pl.when((j >= 0) & (j < outer) & (t > 0))
            def _():
                from_z = nearest(z, j, outer)
                from_x = nearest(x, jnp.int32(i), inner)
                full_copy(h, index(from_z, from_x, c), 4, index(z, x, 1 - c)).wait_recv()
                each_full(h, from_z, from_x, start)

    def multiply(h, t):
        for i in range(inner):
            j = t - 1 - LAG * i

            @pl.when((j >= 0) & (j < outer))
            def _():
                from_z = nearest(z, j, outer)
                from_x = nearest(x, jnp.int32(i), inner)
                full_copy(h, index(from_z, from_x, 1 - c), 4, index(z, x, 1 - c)).wait_recv()
                chip = from_z * inner + from_x
                slot = chip * 2
                right_real = jnp.concatenate([full[h, slot, 0], full[h, slot + 1, 0]], axis=0)
                right_imag = jnp.concatenate([full[h, slot, 1], full[h, slot + 1, 1]], axis=0)
                real, imag = pair_product(a4[chip], right_real, right_imag, rows)
                off_all[h, own, 0] = off_all[h, own, 0] + real
                off_all[h, own, 1] = off_all[h, own, 1] + imag

    def gather(first):
        def step(t, carry):
            for h in range(first, chunks):
                relay(h, t - SKEW * h)
            for h in range(first, chunks):
                multiply(h, t - SKEW * h)
            return carry

        begin = 1 if first == 0 else last + 1 + SKEW * (first - 1)
        lax.fori_loop(begin, last + 1 + SKEW * first, step, 0)

    def finish_rows(h):
        off_real = -off_all[h, own, 0] * live[:, :wide]
        off_imag = -off_all[h, own, 1] * live[:, :wide]
        off_all[h, own, 0] = off_real
        off_all[h, own, 1] = off_imag
        each_off(h, x, start)
        pole_off[h, pole, 0] = weight_real * off_real - weight_imag * off_imag
        pole_off[h, pole, 1] = weight_real * off_imag + weight_imag * off_real
        for k in range(1, poles):
            pole_copy(h, pole_off, po_send, po_recv, pole, (pole + k) % poles, k).start()

    def make_gram(h):
        for i in range(1, inner):
            from_x = nearest(x, jnp.int32(i), inner)
            off_copy(h, index(0, from_x, c), 2, index(z, x, 1 - c)).wait_recv()
            each_off(h, from_x, start)
        for i in range(inner):
            off_copy(h, index(0, i, 1 - c), 2, index(z, x, 1 - c)).wait_recv()
        right_real = jnp.concatenate([off_all[h, k, 0] for k in range(group)], axis=0)
        right_imag = jnp.concatenate([off_all[h, k, 1] for k in range(group)], axis=0)
        gram_real, gram_imag = pair_product(left4[...], right_real, right_imag, outer * share)
        for k in range(outer):
            gram[h, k, 0] = gram_real[k * share : (k + 1) * share]
            gram[h, k, 1] = gram_imag[k * share : (k + 1) * share]
        for k in range(1, outer):
            gram_copy(h, z, (z + k) % outer, k).start()

    def sum_gram(h):
        at = slice(h * wide, (h + 1) * wide)
        real, imag = d_ref[0, :, at] - gram[h, z, 0], d_ref[1, :, at] - gram[h, z, 1]
        for k in range(1, outer):
            from_z = (z + k) % outer
            gram_copy(h, from_z, from_z, k).wait_recv()
            real, imag = real - gram_in[h, from_z, 0], imag - gram_in[h, from_z, 1]
        pole_diag[h, pole, 0] = weight_real * real - weight_imag * imag
        pole_diag[h, pole, 1] = weight_real * imag + weight_imag * real
        for k in range(1, poles):
            pole_copy(h, pole_diag, pd_send, pd_recv, pole, (pole + k) % poles, k).start()

    for h in range(chunks + 2):
        if h < chunks:
            gather(h)
            finish_rows(h)
        if h == 1:
            make_rows()
        if 1 <= h <= chunks:
            make_gram(h - 1)
        if h >= 2:
            sum_gram(h - 2)

    def add_poles(h, buffer, send, recv, out):
        for k in range(1, poles):
            other = (pole + k) % poles
            pole_copy(h, buffer, send, recv, other, other, k).wait_recv()
        total = buffer[h, 0]
        for k in range(1, poles):
            total = total + buffer[h, k]
        out[:, :, h * wide : (h + 1) * wide] = total

    for h in range(chunks):
        add_poles(h, pole_off, po_send, po_recv, off_out)

    def finish(slot, carry):
        for h in range(chunks):
            each_full(h, slot // inner, slot % inner, lambda copy: copy.wait_send())
        return carry

    lax.fori_loop(0, chips, finish, 0)
    for h in range(chunks):
        for i in range(inner):
            each_off(h, jnp.int32(i), lambda copy: copy.wait_send())
        for k in range(1, outer):
            gram_copy(h, z, (z + k) % outer, k).wait_send()
        for k in range(1, poles):
            pole_copy(h, pole_off, po_send, po_recv, pole, (pole + k) % poles, k).wait_send()
    for h in range(chunks):
        add_poles(h, pole_diag, pd_send, pd_recv, diag_out)
        for k in range(1, poles):
            pole_copy(h, pole_diag, pd_send, pd_recv, pole, (pole + k) % poles, k).wait_send()


def per_device(dims, inverse_block, factor_block, diag_inverse, residues, block_owner, row_count):
    poles, outer, inner = dims
    _, _, rows, total_rows = inverse_block.shape
    width = factor_block.shape[3]
    share = diag_inverse.shape[2]
    n, group, chips = outer * inner * 2, inner * 2, outer * inner
    dma = pltpu.SemaphoreType.DMA
    chunks = CHUNKS if width % (128 * CHUNKS) == 0 else 1
    wide = width // chunks
    vmem, smem = pl.BlockSpec(memory_space=pltpu.VMEM), pl.BlockSpec(memory_space=pltpu.SMEM)
    return pl.pallas_call(
        functools.partial(kernel, dims),
        out_shape=(
            jax.ShapeDtypeStruct((2, rows, width), F32),
            jax.ShapeDtypeStruct((2, share, width), F32),
        ),
        in_specs=[vmem, vmem, vmem, smem, smem, smem],
        out_specs=(vmem, vmem),
        scratch_shapes=[
            pltpu.VMEM((chunks, n, 2, rows, wide), F32),
            pltpu.VMEM((chips, 4 * rows, 2 * rows), BF16),
            pltpu.VMEM((chunks, group, 2, rows, wide), F32),
            pltpu.VMEM((2, width, group * rows), F32),
            pltpu.VMEM((4 * outer * share, group * rows), BF16),
            pltpu.VMEM((chunks, outer, 2, share, wide), F32),
            pltpu.VMEM((chunks, outer, 2, share, wide), F32),
            pltpu.VMEM((chunks, poles, 2, rows, wide), F32),
            pltpu.VMEM((chunks, poles, 2, share, wide), F32),
            dma((chunks, n, 5)), dma((chunks, n)), dma((chunks, group, 3)), dma((chunks, group)),
            dma((chunks, outer)), dma((chunks, outer)),
            dma((chunks, poles)), dma((chunks, poles)), dma((chunks, poles)), dma((chunks, poles)),
        ],
        compiler_params=pltpu.CompilerParams(
            collective_id=0, has_side_effects=True, vmem_limit_bytes=56 * 1024 * 1024
        ),
    )(inverse_block[0], factor_block[0], diag_inverse[0], residues[0], block_owner, row_count)


def grid_lines(mesh):
    chips = mesh.shape["grid"] // 2
    inner = max(k for k in range(1, chips + 1) if chips % k == 0 and k * k <= chips)
    try:
        places = [tuple(device.coords) for device in mesh.devices.reshape(mesh.shape["poles"], -1)[0]][::2]
        moved = next(i for i in range(3) if places[1][i] != places[0][i])
        run = len({place[moved] for place in places})
        inner = run if chips % run == 0 else inner
    except (AttributeError, IndexError, StopIteration):
        pass
    return chips // inner, inner


def solution(mesh):
    placed = (
        P("poles", None, "grid", None),
        P("poles", None, "grid", None),
        P("poles", None, "grid", None),
        P("poles", None),
        P(),
        P(),
    )
    dims = (mesh.shape["poles"],) + grid_lines(mesh)
    return jax.shard_map(
        functools.partial(per_device, dims),
        mesh=mesh,
        in_specs=placed,
        out_specs=(P(None, "grid", None), P(None, "grid", None)),
        check_vma=False,
    )
```
